512 devices in a mesh: vel: 16 (over y, z_hi, core), space: 32 (over x, z_lo).
Axes of the slice: x: 4, y: 4, z: 16 (z_hi: 2, z_lo: 8; z = z_hi * 8 + z_lo), core: 2. Of those that a mesh axis runs over, the one named last changes fastest.
Arguments:
- distribution: float32 [16, 256, 16, 16, 256], P('vel', 'space'), as said below
- encounter_frequency_coefficients: float32 [256, 16, 16], P('space'), may hold values from 5 to 60
Outputs:
- relaxed: float32 [16, 256, 16, 16, 256], P('vel', 'space')
The draws below stay inside these ranges and needn't reach their ends.
Inputs may be any that keep to these rules, and one draw needn't show every extreme that they name: `distribution`: every entry is positive.
All inputs are finite; a program needn't handle non-finite values.
Results may differ from the reference program's by a relative error of at most 0.0003.
Values sent between devices are 32-bit elements; how exact they have to be, the bound alone decides.
A program may use at most 64 MiB of HBM per device.

```python
import math
import jax
import jax.numpy as jnp
from jax import lax

NV = 16
NX = 256
NY = 16
NZ = 16


def draw_distribution(key, part):
    key = jax.random.fold_in(key, 11)
    split_keys = jax.random.split(key, 7)
    velocities = (jnp.arange(NV, dtype=jnp.float32) - (NV - 1) / 2.0) * 0.6
    plane_index = jnp.arange(NV * NV)
    speed_x = (((plane_index % NV).astype(jnp.float32) - (NV - 1) / 2.0) * 0.6).reshape(1, 1, 1, 1, -1)
    speed_y = (((plane_index // NV).astype(jnp.float32) - (NV - 1) / 2.0) * 0.6).reshape(1, 1, 1, 1, -1)
    speed_z = velocities.reshape(-1, 1, 1, 1, 1)
    cell_shape = (1, NX, NY, NZ, 1)
    warmth = jnp.exp(jax.random.uniform(split_keys[0], cell_shape, jnp.float32, math.log(0.7), math.log(1.4)))
    roughness = jnp.exp(jax.random.uniform(split_keys[1], (NV, NX, NY, NZ, NV * NV), jnp.float32, math.log(0.5), math.log(2.0)))
    skew_x = jax.random.uniform(split_keys[4], cell_shape, jnp.float32, -0.25, 0.25)
    skew_y = jax.random.uniform(split_keys[5], cell_shape, jnp.float32, -0.25, 0.25)
    skew_z = jax.random.uniform(split_keys[6], cell_shape, jnp.float32, -0.25, 0.25)
    drift_x = jnp.zeros(cell_shape, jnp.float32)
    rel_x = speed_x - drift_x
    spread = rel_x ** 2 + speed_y ** 2 + speed_z ** 2
    along_skew = (skew_x * rel_x + skew_y * speed_y + skew_z * speed_z) / jnp.sqrt(warmth)
    tilt = jnp.maximum(1.0 + along_skew * (spread / warmth - 5.0) / 5.0, 0.2)
    return roughness * tilt * jnp.exp(-spread / (2.0 * warmth)) / warmth ** 1.5


def block_scale(stream_key, dims, shards, smallest, top_value):
    gain, own = 1.0, jax.random.fold_in(stream_key, 6)
    for dim, shards_of in shards:
        steps = jnp.exp(jax.random.uniform(jax.random.fold_in(own, dim), (shards_of,), jnp.float32, smallest / len(shards), top_value / len(shards)))
        gain = gain * jnp.repeat(steps, dims[dim] // shards_of).reshape([-1 if axis == dim else 1 for axis in range(len(dims))])
    return gain


def setup_inputs(seed: int = 0) -> dict:
    key_of = jax.random.split(jax.random.key(seed), 3)
    return {
        "distribution": draw_distribution(jax.random.fold_in(key_of[2], 71), 0),
        "encounter_frequency_coefficients": jnp.clip(jnp.exp(math.log(60.0) - 2.4849066 * jax.random.uniform(key_of[1], (NX, NY, NZ), jnp.float32) ** block_scale(key_of[1], (NX, NY, NZ), ((0, 32),), -0.2, 0.2)), 5.0, 60.0),
    }


dv_step = 0.6
explicit_stepsize = 0.035
prandtl = 2.0 / 3.0
shear_power_law_index = 0.81
discrete_speed_points = dv_step ** 3 / (2.0 * math.pi) ** 1.5


def minmod(first, second):
    return 0.5 * (jnp.sign(first) + jnp.sign(second)) * jnp.minimum(jnp.abs(first), jnp.abs(second))


def cut(array, begin, finish, along):
    return lax.slice_in_dim(array, begin, finish, axis=along)


def divergence(padded, speed, along):
    length = padded.shape[along] - 4
    jumps = cut(padded, 1, length + 4, along) - cut(padded, 0, length + 3, along)
    slopes = minmod(cut(jumps, 0, length + 2, along), cut(jumps, 1, length + 3, along))
    center = cut(padded, 1, length + 3, along)
    upper = center + 0.5 * slopes
    lower = center - 0.5 * slopes
    fluxes = jnp.maximum(speed, 0.0) * cut(upper, 0, length + 1, along) + jnp.minimum(speed, 0.0) * cut(lower, 1, length + 2, along)
    return cut(fluxes, 1, length + 1, along) - cut(fluxes, 0, length, along)


def reference(distribution, encounter_frequency_coefficients):
    velocities = (jnp.arange(NV, dtype=jnp.float32) - (NV - 1) / 2.0) * dv_step
    plane_index = jnp.arange(NV * NV)
    speed_x = (((plane_index % NV).astype(jnp.float32) - (NV - 1) / 2.0) * dv_step).reshape(1, 1, 1, -1)
    speed_y = (((plane_index // NV).astype(jnp.float32) - (NV - 1) / 2.0) * dv_step).reshape(1, 1, 1, -1)
    mirror_walls = distribution[::-1, :, :, 0:2, :]

    def advect(items):
        plane_field, mirror_wall, speed_z = items
        x_padded = jnp.concatenate([plane_field[-2:], plane_field, plane_field[:2]], axis=0)
        y_padded = jnp.concatenate([plane_field[:, -2:], plane_field, plane_field[:, :2]], axis=1)
        top_row = plane_field[:, :, -1:, :]
        z_padded = jnp.concatenate([mirror_wall[:, :, ::-1, :], plane_field, top_row, top_row], axis=2)
        change = divergence(x_padded, speed_x, 0) + divergence(y_padded, speed_y, 1) + divergence(z_padded, speed_z, 2)
        return plane_field - explicit_stepsize * change

    moved = lax.map(advect, (distribution, mirror_walls, velocities))

    def first_sums(carry, items):
        plane_field, speed_z = items
        mass = jnp.sum(plane_field, axis=-1)
        return (carry[0] + mass, carry[1] + jnp.sum(plane_field * speed_x, axis=-1),
                carry[2] + jnp.sum(plane_field * speed_y, axis=-1), carry[3] + speed_z * mass), None

    zero_cells = jnp.zeros((NX, NY, NZ), jnp.float32)
    sums, _ = lax.scan(first_sums, (zero_cells, zero_cells, zero_cells, zero_cells), (moved, velocities))
    particle_concentration = discrete_speed_points * sums[0]
    flow_x = discrete_speed_points * sums[1] / particle_concentration
    flow_y = discrete_speed_points * sums[2] / particle_concentration
    flow_z = discrete_speed_points * sums[3] / particle_concentration
    rel_x = speed_x - flow_x[..., None]
    rel_y = speed_y - flow_y[..., None]

    def second_sums(carry, items):
        plane_field, speed_z = items
        rel_z = speed_z - flow_z[..., None]
        rel_sq = rel_x * rel_x + rel_y * rel_y + rel_z * rel_z
        weighted = rel_sq * plane_field
        return (carry[0] + jnp.sum(weighted, axis=-1), carry[1] + jnp.sum(rel_x * weighted, axis=-1),
                carry[2] + jnp.sum(rel_y * weighted, axis=-1), carry[3] + jnp.sum(rel_z * weighted, axis=-1)), None

    thermal_current_components, _ = lax.scan(second_sums, (zero_cells, zero_cells, zero_cells, zero_cells), (moved, velocities))
    kinetic_warmth_field = discrete_speed_points * thermal_current_components[0] / (3.0 * particle_concentration)
    heat_x = 0.5 * discrete_speed_points * thermal_current_components[1]
    heat_y = 0.5 * discrete_speed_points * thermal_current_components[2]
    heat_z = 0.5 * discrete_speed_points * thermal_current_components[3]
    relaxation_multiplier = jnp.exp(-explicit_stepsize * encounter_frequency_coefficients * particle_concentration * kinetic_warmth_field ** (1.0 - shear_power_law_index))

    def relax(items):
        plane_field, speed_z = items
        rel_z = speed_z - flow_z[..., None]
        rel_sq = rel_x * rel_x + rel_y * rel_y + rel_z * rel_z
        shakhov_corrected_distribution = kinetic_warmth_field[..., None]
        maxwell = particle_concentration[..., None] * shakhov_corrected_distribution ** -1.5 * jnp.exp(-rel_sq / (2.0 * shakhov_corrected_distribution))
        along_heat = rel_x * heat_x[..., None] + rel_y * heat_y[..., None] + rel_z * heat_z[..., None]
        target = maxwell * (1.0 + (1.0 - prandtl) * along_heat / (5.0 * particle_concentration[..., None] * shakhov_corrected_distribution * shakhov_corrected_distribution) * (rel_sq / shakhov_corrected_distribution - 5.0))
        return target + (plane_field - target) * relaxation_multiplier[..., None]

    return lax.map(relax, (moved, velocities))
```

```python
import functools
import math

import jax
import jax.numpy as jnp
import numpy as np
from jax import lax
from jax.experimental import pallas as pl
from jax.experimental.pallas import tpu as pltpu
from jax.sharding import PartitionSpec as P

NV = 16
UNIT = 0.3
DT = 0.035
WEIGHT = 0.6**3 / (2.0 * math.pi) ** 1.5
MESH = pl.DeviceIdType.MESH
F32 = jnp.float32
BF16 = jnp.bfloat16

HALO, WALL, SCAT, CROSS, GATH, WCROSS, WCAST, COPIES = 0, 4, 8, 16, 17, 25, 26, 34


def minmod(p, q):
    return jnp.maximum(jnp.minimum(p, q), 0.0) + jnp.minimum(jnp.maximum(p, q), 0.0)


def basis_table():
    b = np.arange(256)
    x, y = 2.0 * (b % 16) - 15, 2.0 * (b // 16) - 15
    one = np.ones(256)
    rows = [(0, one), (0, x), (0, y), (0, x * x), (0, y * y), (1, one), (1, x), (1, y), (2, one), (3, one)]
    table = np.zeros((32, 1024), np.float32)
    for part in range(3):
        for k, (block, values) in enumerate(rows):
            table[part * 10 + k, block * 256 : block * 256 + 256] = values
    return table


def cell_values(m, nu):
    mass, sx, sy, sz, xx, yy, zz, xy, xz, yz = (m[k : k + 1] for k in range(10))
    cx, cy, cz = (m[k : k + 1] + m[k + 3 : k + 4] for k in range(10, 13))
    inv = 1.0 / mass
    ux, uy, uz = sx * inv, sy * inv, sz * inv
    energy = xx + yy + zz
    dot = ux * sx + uy * sy + uz * sz
    sq = ux * ux + uy * uy + uz * uz
    kinetic = energy - 2.0 * dot + sq * mass
    common = 2.0 * dot - energy - sq * mass
    fx = cx - 2.0 * (ux * xx + uy * xy + uz * xz) + ux * common + sq * sx
    fy = cy - 2.0 * (ux * xy + uy * yy + uz * yz) + uy * common + sq * sy
    fz = cz - 2.0 * (ux * xz + uy * yz + uz * zz) + uz * common + sq * sz
    temp = (UNIT * UNIT / 3.0) * kinetic * inv
    dens = WEIGHT * mass
    log_t = jnp.log(temp)
    decay = jnp.exp(-DT * nu * dens * jnp.exp((1.0 - 0.81) * log_t))
    inv_t = 1.0 / temp
    scale = (1.0 - decay) * dens * inv_t * lax.rsqrt(temp)
    skew = (1.0 - 2.0 / 3.0) / 5.0 * (0.5 * WEIGHT * UNIT**4) * scale / dens * inv_t * inv_t
    return ux, uy, uz, (UNIT * UNIT) * inv_t, scale, skew * fx, skew * fy, skew * fz, decay


def relax(rows, basis, moved, vz):
    ux, uy, uz, rt, scale, kx, ky, kz, decay = rows
    cz = vz - uz
    coef = [
        rt * (ux * ux + uy * uy + cz * cz),
        -2.0 * rt * ux,
        -2.0 * rt * uy,
        rt,
        rt,
        kz * cz - kx * ux - ky * uy,
        kx,
        ky,
        scale,
        decay,
    ]
    coef = jnp.concatenate(coef, axis=0)
    hi = coef.astype(BF16).astype(F32)
    mid = (coef - hi).astype(BF16).astype(F32)
    low = coef - hi - mid
    stacked = jnp.concatenate([hi, mid, low, jnp.zeros((2, coef.shape[1]), F32)], axis=0)
    left = stacked.T.astype(BF16)
    wide = jnp.dot(left, basis, preferred_element_type=F32)
    rr = wide[:, 0:256]
    return jnp.exp(-0.5 * rr) * (wide[:, 512:768] + wide[:, 256:512] * (rr - 5.0)) + moved * wide[:, 768:1024]


def kernel(f_hbm, nu_ref, nuw_ref, basis_ref, out_hbm, g, acc, hp, xf, xp, ws, wr, mom, rs, zr, par, wm, wo, ws_mom, wz, wb, send, recv, local):
    vel, space = lax.axis_index("vel"), lax.axis_index("space")
    n_space = lax.axis_size("space")
    vy, zh, core = vel // 4, (vel // 2) % 2, vel % 2
    grp = vy * 2 + core

    def peer(o):
        p = (grp + o) % 8
        return {"vel": (p // 2) * 4 + zh * 2 + p % 2, "space": space}

    up = {"vel": vel, "space": (space + 1) % n_space}
    down = {"vel": vel, "space": (space + n_space - 1) % n_space}
    mirror = {"vel": NV - 1 - vel, "space": space}
    across = {"vel": vel + 2 - 4 * zh, "space": space}
    plus = vel >= NV // 2

    barrier = pltpu.get_barrier_semaphore()
    friends = [up, down, mirror, across] + [peer(o) for o in range(1, 8)]
    for d in friends:
        pl.semaphore_signal(barrier, inc=1, device_id=d, device_id_type=MESH)

    order = [0, 1, 6, 7, 2, 3, 4, 5]
    def halves(x):
        return [(f_hbm.at[x, :, pl.ds(h * 128, 128)], g.at[x, h], local.at[x, h]) for h in range(2)]

    loads = [[pltpu.make_async_copy(*c) for c in halves(x)] for x in range(8)]
    for x in order:
        for cp in loads[x]:
            cp.start()

    def remote(src, dst, k, dev):
        return pltpu.make_async_remote_copy(src, dst, send.at[k], recv.at[k], device_id=dev, device_id_type=MESH)

    vz = (2 * vel - 15).astype(F32)
    lane = lax.broadcasted_iota(jnp.int32, (8, 128), 1)
    sub = lax.broadcasted_iota(jnp.int32, (8, 128), 0)
    vx = (2 * (lane % 16) - 15).astype(F32)
    xpos = lane % 16 >= 8
    step_x = -DT * UNIT * vx
    step_y = [-DT * UNIT * (2 * (lane // 16 + 8 * h) - 15).astype(F32) for h in range(2)]

    for x in order[:4]:
        for cp in loads[x]:
            cp.wait()

    def pack(t, _):
        for h in range(2):
            near, far = pl.ds(pl.multiple_of(t * 8, 8), 8), pl.ds(pl.multiple_of(t * 8 + 128, 8), 8)
            hp[0, h, near] = jnp.where(xpos, g[6, h, near], pltpu.roll(g[6, h, far], 120, 1))
            hp[1, h, near] = jnp.where(xpos, pltpu.roll(g[1, h, far], 8, 1), g[1, h, near])
        return 0

    lax.fori_loop(0, 16, pack, 0)
    pl.semaphore_wait(barrier, len(friends))
    halo = [
        remote(g.at[7], xf.at[0], HALO, up),
        remote(g.at[0], xf.at[1], HALO + 1, down),
        remote(hp.at[0], xp.at[0], HALO + 2, up),
        remote(hp.at[1], xp.at[1], HALO + 3, down),
    ]
    for cp in halo:
        cp.start()
    for x in order[4:]:
        for cp in loads[x]:
            cp.wait()

    def pack_wall(x, _):
        for l in range(2):
            for h in range(2):
                ws[l, x, h] = g[x, h, pl.ds(l, 16, stride=16), :]
        return 0

    lax.fori_loop(0, 8, pack_wall, 0)
    wall = [remote(ws.at[0, pl.ds(4 * k, 4)], wr.at[0, pl.ds(4 * k, 4)], WALL + k, mirror) for k in range(2)]
    wall2 = [remote(ws.at[1, pl.ds(4 * k, 4)], wr.at[1, pl.ds(4 * k, 4)], WALL + 2 + k, mirror) for k in range(2)]
    for cp in wall:
        cp.start()

    @pl.when(jnp.logical_not(plus))
    def _():
        for cp in wall2:
            cp.start()

    def local_pass(positive):
        cz = -DT * UNIT * vz
        cz0 = jnp.where(sub < (2 if positive else 1), 0.0, cz)

        def body(x, _):
            for h in range(2):
                for t in range(2):
                    v = [g[x, h, k * 16 + t * 8 : k * 16 + t * 8 + 8] for k in range(16)]
                    d = [v[k] - v[k - 1] for k in range(16)]
                    half = [0.5 * minmod(d[k], d[(k + 1) % 16]) for k in range(16)]
                    if h:
                        u = [v[k] + half[k] for k in range(16)]
                        change = [u[k] - u[k - 1] for k in range(16)]
                    else:
                        u = [v[k] - half[k] for k in range(16)]
                        change = [u[(k + 1) % 16] - u[k] for k in range(16)]
                    for k in range(16):
                        acc[x, h, k * 16 + t * 8 : k * 16 + t * 8 + 8] = v[k] + step_y[h] * change[k]
                for k in range(16):
                    r0, r1 = pl.ds(k * 16, 8), pl.ds(k * 16 + 8, 8)
                    t0, t1 = g[x, h, r0], g[x, h, r1]
                    b0, b1 = pltpu.roll(t0, 1, 0), pltpu.roll(t1, 1, 0)
                    d0, d1 = t0 - b0, t1 - jnp.where(sub == 0, b0, b1)
                    a0, a1 = pltpu.roll(d0, 7, 0), pltpu.roll(d1, 7, 0)
                    m0 = 0.5 * minmod(d0, jnp.where(sub == 7, a1, a0))
                    m1 = 0.5 * minmod(d1, jnp.where(sub == 7, 0.0, a1))
                    if positive:
                        u0, u1 = t0 + m0, t1 + m1
                        s0, s1 = pltpu.roll(u0, 1, 0), pltpu.roll(u1, 1, 0)
                        e0, e1 = u0 - s0, u1 - jnp.where(sub == 0, s0, s1)
                    else:
                        u0, u1 = t0 - m0, t1 - m1
                        s0, s1 = pltpu.roll(u0, 7, 0), pltpu.roll(u1, 7, 0)
                        e0, e1 = jnp.where(sub == 7, s1, s0) - u0, jnp.where(sub == 7, t1, s1) - u1
                    acc[x, h, r0] += cz0 * e0
                    acc[x, h, r1] += cz * e1
            return 0

        lax.fori_loop(0, 8, body, 0)

    pl.when(plus)(lambda: local_pass(True))
    pl.when(jnp.logical_not(plus))(lambda: local_pass(False))

    for cp in halo:
        cp.wait_recv()

    def x_pass(t, _):
        near, far = pl.ds(pl.multiple_of(t * 8, 8), 8), pl.ds(pl.multiple_of(t * 8 + 128, 8), 8)
        for h in range(2):
            for k, rows in enumerate((near, far)):
                low, high = xp[0, h, near], xp[1, h, near]
                if k:
                    low, high = pltpu.roll(low, 8, 1), pltpu.roll(high, 120, 1)
                v = [low, xf[0, h, rows]] + [g[x, h, rows] for x in range(8)] + [xf[1, h, rows], high]
                d = [v[i + 1] - v[i] for i in range(11)]
                half = [0.5 * minmod(d[i], d[i + 1]) for i in range(10)]
                face = [jnp.where(xpos, v[i + 1] + half[i], v[i + 2] - half[i + 1]) for i in range(9)]
                for x in range(8):
                    acc[x, h, rows] += step_x * (face[x + 1] - face[x])
        return 0

    lax.fori_loop(0, 16, x_pass, 0)

    row = lax.broadcasted_iota(jnp.int32, (16, 256), 0)
    b = lax.broadcasted_iota(jnp.int32, (16, 256), 1)
    wx, wy = (2 * (b % 16) - 15).astype(F32), (2 * (b // 16) - 15).astype(F32)
    wz_ = jnp.zeros((16, 256), F32) + vz
    cube = wx * wx + wy * wy + wz_ * wz_
    table = [jnp.ones_like(wx), wx, wy, wz_, wx * wx, wy * wy, wz_ * wz_, wx * wy, wx * wz_, wy * wz_, wx * cube, wy * cube, wz_ * cube]
    weight = table[0]
    for k in range(1, 16):
        entry = table[k] if k < 13 else table[k - 3] - table[k - 3].astype(BF16).astype(F32)
        weight = jnp.where(row == k, entry, weight)
    weight = weight.astype(BF16)

    def sums(cells):
        hi = cells.astype(BF16)
        low = (cells - hi.astype(F32)).astype(BF16)
        dims = (((1,), (1,)), ((), ()))
        return lax.dot_general(weight, hi, dims, preferred_element_type=F32) + lax.dot_general(
            weight, low, dims, preferred_element_type=F32
        )

    def joined(ref, x):
        return jnp.concatenate([ref[x, 0], ref[x, 1]], axis=1)

    def main_sums(x, _):
        mom[x] = sums(joined(acc, x))
        return 0

    lax.fori_loop(0, 8, main_sums, 0)

    scatter = [remote(mom.at[(grp + o) % 8], rs.at[o], SCAT + o, peer(o)) for o in range(1, 8)]
    for cp in scatter:
        cp.start()
    total = mom[grp]
    for cp in scatter:
        cp.wait_recv()
    for o in range(1, 8):
        total = total + rs[o]
    zr[0] = total
    cross = remote(zr.at[0], zr.at[1], CROSS, across)
    cross.start()

    for cp in wall:
        cp.wait_recv()

    def wall_pass(positive):
        cz = -DT * UNIT * vz

        def body(x, _):
            for h in range(2):
                v0, v1, v2 = (g[x, h, pl.ds(l, 16, stride=16), :] for l in range(3))
                w0, d1 = wr[0, x, h], v1 - v0
                d0, m1 = v0 - w0, 0.5 * minmod(d1, v2 - v1)
                m0 = 0.5 * minmod(d0, d1)
                a0, a1 = (acc[x, h, pl.ds(l, 16, stride=16), :] for l in range(2))
                if positive:
                    bottom = w0 + 0.5 * minmod(w0 - wr[1, x, h], d0)
                    u0, u1 = v0 + m0, v1 + m1
                    a0, a1 = a0 + cz * (u0 - bottom), a1 + cz * (u1 - u0)
                else:
                    a0 = a0 + cz * ((v1 - m1) - (v0 - m0))
                wm[h, x, 0:16] = a0
                wm[h, x, 16:32] = a1
            return 0

        lax.fori_loop(0, 8, body, 0)

    @pl.when(plus)
    def _():
        for cp in wall2:
            cp.wait_recv()
        wall_pass(True)

    pl.when(jnp.logical_not(plus))(lambda: wall_pass(False))
    beside = jnp.concatenate([wm[0].reshape(256, 128), wm[1].reshape(256, 128)], axis=1)
    ws_mom[0] = sums(beside)
    wcross = remote(ws_mom.at[0], wz.at[0], WCROSS, across)
    wcross.start()

    cross.wait_recv()
    rows = cell_values(total + zr[1], nu_ref[grp])
    par[grp] = jnp.concatenate(list(rows) + [jnp.zeros((7, 256), F32)], axis=0)
    gather = [remote(par.at[grp], par.at[grp], GATH + o, peer(o)) for o in range(1, 8)]
    for cp in gather:
        cp.start()
    for cp in gather:
        cp.wait_recv()

    basis = basis_ref[...].astype(BF16)

    def main_relax(x, _):
        table = par[x]
        out = relax([table[k : k + 1] for k in range(9)], basis, joined(acc, x), vz)
        for h in range(2):
            acc[x, h] = out[:, h * 128 : h * 128 + 128]
        return 0

    lax.fori_loop(0, 8, main_relax, 0)

    wcross.wait_recv()
    wb[0] = ws_mom[0] + wz[0]
    cast = [remote(wb.at[0], wb.at[o], WCAST + o, peer(o)) for o in range(1, 8)]
    for cp in cast:
        cp.start()
    for cp in cast:
        cp.wait_recv()
    total = wb[0]
    for o in range(1, 8):
        total = total + wb[o]
    out = relax(cell_values(total, nuw_ref[...]), basis, beside, vz)
    for h in range(2):
        wo[h] = out[:, h * 128 : h * 128 + 128].reshape(8, 32, 128)

    def place(x, _):
        for l in range(2):
            for h in range(2):
                acc[x, h, pl.ds(l, 16, stride=16), :] = wo[h, x, l * 16 : l * 16 + 16]
        return 0

    lax.fori_loop(0, 8, place, 0)
    stores = [
        pltpu.make_async_copy(acc.at[x, h], out_hbm.at[x, :, pl.ds(h * 128, 128)], local.at[x, h])
        for x in range(8)
        for h in range(2)
    ]
    for cp in stores:
        cp.start()
    for cp in halo + wall + scatter + [cross, wcross] + gather + cast:
        cp.wait_send()

    @pl.when(jnp.logical_not(plus))
    def _():
        for cp in wall2:
            cp.wait_send()

    for cp in stores:
        cp.wait()


def shards(distribution, coefficients):
    cells = distribution.reshape(8, 256, 256)
    nu = coefficients.reshape(8, 1, 256)
    nu_wall = coefficients[:, :, 0:2].transpose(0, 2, 1).reshape(1, 256)
    vmem, anywhere = pl.BlockSpec(memory_space=pltpu.VMEM), pl.BlockSpec(memory_space=pl.ANY)
    out = pl.pallas_call(
        kernel,
        out_shape=jax.ShapeDtypeStruct((8, 256, 256), F32),
        in_specs=[anywhere, vmem, vmem, vmem],
        out_specs=anywhere,
        scratch_shapes=[
            pltpu.VMEM((8, 2, 256, 128), F32),
            pltpu.VMEM((8, 2, 256, 128), F32),
            pltpu.VMEM((2, 2, 128, 128), F32),
            pltpu.VMEM((2, 2, 256, 128), F32),
            pltpu.VMEM((2, 2, 128, 128), F32),
            pltpu.VMEM((2, 8, 2, 16, 128), F32),
            pltpu.VMEM((2, 8, 2, 16, 128), F32),
            pltpu.VMEM((8, 16, 256), F32),
            pltpu.VMEM((8, 16, 256), F32),
            pltpu.VMEM((2, 16, 256), F32),
            pltpu.VMEM((8, 16, 256), F32),
            pltpu.VMEM((2, 8, 32, 128), F32),
            pltpu.VMEM((2, 8, 32, 128), F32),
            pltpu.VMEM((1, 16, 256), F32),
            pltpu.VMEM((1, 16, 256), F32),
            pltpu.VMEM((8, 16, 256), F32),
            pltpu.SemaphoreType.DMA((COPIES,)),
            pltpu.SemaphoreType.DMA((COPIES,)),
            pltpu.SemaphoreType.DMA((8, 2)),
        ],
        compiler_params=pltpu.CompilerParams(
            collective_id=0, has_side_effects=True, vmem_limit_bytes=40 * 1024 * 1024
        ),
        cost_estimate=pl.CostEstimate(flops=10**8, bytes_accessed=4 * 2**20, transcendentals=2**19),
    )(cells, nu, nu_wall, jnp.asarray(basis_table()))
    return out.reshape(distribution.shape)


def solution(mesh):
    in_specs = (P("vel", "space", None, None, None), P("space", None, None))
    out_specs = P("vel", "space", None, None, None)
    return jax.shard_map(shards, mesh=mesh, in_specs=in_specs, out_specs=out_specs, check_vma=False)
```

```python
import math

import jax
import jax.numpy as jnp
from jax import lax
from jax.experimental import pallas as pl
from jax.experimental.pallas import tpu as pltpu
from jax.sharding import PartitionSpec as P

NV = 16
UNIT = 0.3
DT = 0.035
WEIGHT = 0.6**3 / (2.0 * math.pi) ** 1.5
MESH = pl.DeviceIdType.MESH
F32 = jnp.float32
BF16 = jnp.bfloat16

HALO, WALL, SCAT, CROSS, GATH, PRE, CAST, COPIES = 0, 4, 8, 16, 17, 25, 26, 34


def minmod(p, q):
    return jnp.maximum(jnp.minimum(p, q), 0.0) + jnp.minimum(jnp.maximum(p, q), 0.0)


def basis_table():
    row = lax.broadcasted_iota(jnp.int32, (32, 1024), 0)
    col = lax.broadcasted_iota(jnp.int32, (32, 1024), 1)
    b, block, k = col % 256, col // 256, row % 10
    x, y = (2 * (b % 16) - 15).astype(F32), (2 * (b // 16) - 15).astype(F32)
    value = jnp.where((k == 1) | (k == 6), x, 1.0)
    value = jnp.where((k == 2) | (k == 7), y, value)
    value = jnp.where(k == 3, x * x, jnp.where(k == 4, y * y, value))
    wanted = jnp.where(k < 5, 0, jnp.where(k < 8, 1, k - 6))
    return jnp.where((block == wanted) & (row < 30), value, 0.0).astype(BF16)


def spread(tile, width):
    k, c = (lax.broadcasted_iota(jnp.int32, (16, 256), d) for d in range(2))
    pick = jnp.where(c % width == k, 1.0, 0.0)
    wide = jnp.dot(tile, pick, precision=lax.Precision.HIGHEST, preferred_element_type=F32)
    r, c = (lax.broadcasted_iota(jnp.int32, wide.shape, d) for d in range(2))
    return jnp.sum(jnp.where(r == c // width, wide, 0.0), axis=0, keepdims=True)


def sum_weights(vz):
    row = lax.broadcasted_iota(jnp.int32, (16, 256), 0)
    b = lax.broadcasted_iota(jnp.int32, (16, 256), 1)
    x, y = (2 * (b % 16) - 15).astype(F32), (2 * (b // 16) - 15).astype(F32)
    z = jnp.zeros((16, 256), F32) + vz
    sq = x * x + y * y + z * z
    table = [jnp.ones_like(x), x, y, z, x * x, y * y, z * z, x * y, x * z, y * z, x * sq, y * sq, z * sq]
    weight = table[0]
    for k in range(1, 16):
        entry = table[k] if k < 13 else table[k - 3] - table[k - 3].astype(BF16).astype(F32)
        weight = jnp.where(row == k, entry, weight)
    return weight.astype(BF16)


def sums(weight, cells):
    hi = cells.astype(BF16)
    low = (cells - hi.astype(F32)).astype(BF16)
    dims = (((1,), (1,)), ((), ()))
    return lax.dot_general(weight, hi, dims, preferred_element_type=F32) + lax.dot_general(
        weight, low, dims, preferred_element_type=F32
    )


def joined(ref, x):
    return jnp.concatenate([ref[x, 0], ref[x, 1]], axis=1)


def flat(ref):
    return jnp.concatenate([ref[0].reshape(256, 128), ref[1].reshape(256, 128)], axis=1)


def cell_values(m, nu):
    mass, sx, sy, sz, xx, yy, zz, xy, xz, yz = (m[k : k + 1] for k in range(10))
    cx, cy, cz = (m[k : k + 1] + m[k + 3 : k + 4] for k in range(10, 13))
    inv = 1.0 / mass
    ux, uy, uz = sx * inv, sy * inv, sz * inv
    energy = xx + yy + zz
    dot = ux * sx + uy * sy + uz * sz
    sq = ux * ux + uy * uy + uz * uz
    kinetic = energy - 2.0 * dot + sq * mass
    common = 2.0 * dot - energy - sq * mass
    fx = cx - 2.0 * (ux * xx + uy * xy + uz * xz) + ux * common + sq * sx
    fy = cy - 2.0 * (ux * xy + uy * yy + uz * yz) + uy * common + sq * sy
    fz = cz - 2.0 * (ux * xz + uy * yz + uz * zz) + uz * common + sq * sz
    temp = (UNIT * UNIT / 3.0) * kinetic * inv
    dens = WEIGHT * mass
    log_t = jnp.log(temp)
    decay = jnp.exp(-DT * nu * dens * jnp.exp((1.0 - 0.81) * log_t))
    inv_t = 1.0 / temp
    scale = (1.0 - decay) * dens * inv_t * lax.rsqrt(temp)
    skew = (1.0 - 2.0 / 3.0) / 5.0 * (0.5 * WEIGHT * UNIT**4) * scale / dens * inv_t * inv_t
    return ux, uy, uz, (UNIT * UNIT) * inv_t, scale, skew * fx, skew * fy, skew * fz, decay


def relax(rows, basis, moved, vz):
    ux, uy, uz, rt, scale, kx, ky, kz, decay = rows
    cz = vz - uz
    coef = [
        rt * (ux * ux + uy * uy + cz * cz),
        -2.0 * rt * ux,
        -2.0 * rt * uy,
        rt,
        rt,
        kz * cz - kx * ux - ky * uy,
        kx,
        ky,
        scale,
        decay,
    ]
    coef = jnp.concatenate(coef, axis=0)
    hi = coef.astype(BF16).astype(F32)
    mid = (coef - hi).astype(BF16).astype(F32)
    low = coef - hi - mid
    stacked = jnp.concatenate([hi, mid, low, jnp.zeros((2, coef.shape[1]), F32)], axis=0)
    left = stacked.T.astype(BF16)
    wide = jnp.dot(left, basis, preferred_element_type=F32)
    rr = wide[:, 0:256]
    return jnp.exp(-0.5 * rr) * (wide[:, 512:768] + wide[:, 256:512] * (rr - 5.0)) + moved * wide[:, 768:1024]


def kernel(f_hbm, nu_hbm, out, g, acc, nu, hp, xf, xp, ws, wr, mom, rs, zr, par, wm, dp, dm, pre, cast, send, recv, local, nu_sem):
    vel, space = lax.axis_index("vel"), lax.axis_index("space")
    n_space = lax.axis_size("space")
    vy, zh, core = vel // 4, (vel // 2) % 2, vel % 2
    grp = vy * 2 + core

    def peer(o):
        p = (grp + o) % 8
        return {"vel": (p // 2) * 4 + zh * 2 + p % 2, "space": space}

    up = {"vel": vel, "space": (space + 1) % n_space}
    down = {"vel": vel, "space": (space + n_space - 1) % n_space}
    mirror = {"vel": NV - 1 - vel, "space": space}
    across = {"vel": vel + 2 - 4 * zh, "space": space}
    plus = vel >= NV // 2

    barrier = pltpu.get_barrier_semaphore()
    friends = [up, down, mirror, across] + [peer(o) for o in range(1, 8)]
    for d in friends:
        pl.semaphore_signal(barrier, inc=1, device_id=d, device_id_type=MESH)

    order = [0, 1, 6, 7, 2, 3, 4, 5]
    def halves(x):
        return [(f_hbm.at[x, :, pl.ds(h * 128, 128)], g.at[x, h], local.at[x, h]) for h in range(2)]

    loads = [[pltpu.make_async_copy(*c) for c in halves(x)] for x in range(8)]
    for x in order:
        for cp in loads[x]:
            cp.start()

    load_nu = pltpu.make_async_copy(nu_hbm, nu, nu_sem)
    load_nu.start()

    def remote(src, dst, k, dev):
        return pltpu.make_async_remote_copy(src, dst, send.at[k], recv.at[k], device_id=dev, device_id_type=MESH)

    vz = (2 * vel - 15).astype(F32)
    lane = lax.broadcasted_iota(jnp.int32, (8, 128), 1)
    sub = lax.broadcasted_iota(jnp.int32, (8, 128), 0)
    vx = (2 * (lane % 16) - 15).astype(F32)
    xpos = lane % 16 >= 8
    step_x = -DT * UNIT * vx
    step_y = [-DT * UNIT * (2 * (lane // 16 + 8 * h) - 15).astype(F32) for h in range(2)]

    for x in order[:4]:
        for cp in loads[x]:
            cp.wait()

    def pack(t, _):
        for h in range(2):
            near, far = pl.ds(pl.multiple_of(t * 8, 8), 8), pl.ds(pl.multiple_of(t * 8 + 128, 8), 8)
            hp[0, h, near] = jnp.where(xpos, g[6, h, near], pltpu.roll(g[6, h, far], 120, 1))
            hp[1, h, near] = jnp.where(xpos, pltpu.roll(g[1, h, far], 8, 1), g[1, h, near])
        return 0

    lax.fori_loop(0, 16, pack, 0)
    pl.semaphore_wait(barrier, len(friends))
    halo = [
        remote(g.at[7], xf.at[0], HALO, up),
        remote(g.at[0], xf.at[1], HALO + 1, down),
        remote(hp.at[0], xp.at[0], HALO + 2, up),
        remote(hp.at[1], xp.at[1], HALO + 3, down),
    ]
    for cp in halo:
        cp.start()
    for x in order[4:]:
        for cp in loads[x]:
            cp.wait()

    def pack_wall(x, _):
        for l in range(2):
            for h in range(2):
                ws[l, x, h] = g[x, h, pl.ds(l, 16, stride=16), :]
        return 0

    lax.fori_loop(0, 8, pack_wall, 0)
    wall = [remote(ws.at[l], wr.at[l], WALL + l, mirror) for l in range(2)]
    for cp in wall:
        cp.start()

    def local_pass(positive):
        cz = -DT * UNIT * vz
        cz0 = jnp.where(sub < 1, 0.0, cz) if positive else cz

        def body(x, _):
            for h in range(2):
                for t in range(2):
                    v = [g[x, h, k * 16 + t * 8 : k * 16 + t * 8 + 8] for k in range(16)]
                    d = [v[k] - v[k - 1] for k in range(16)]
                    half = [0.5 * minmod(d[k], d[(k + 1) % 16]) for k in range(16)]
                    if h:
                        u = [v[k] + half[k] for k in range(16)]
                        change = [u[k] - u[k - 1] for k in range(16)]
                    else:
                        u = [v[k] - half[k] for k in range(16)]
                        change = [u[(k + 1) % 16] - u[k] for k in range(16)]
                    for k in range(16):
                        acc[x, h, k * 16 + t * 8 : k * 16 + t * 8 + 8] = v[k] + step_y[h] * change[k]
                for k in range(16):
                    r0, r1 = pl.ds(k * 16, 8), pl.ds(k * 16 + 8, 8)
                    t0, t1 = g[x, h, r0], g[x, h, r1]
                    b0, b1 = pltpu.roll(t0, 1, 0), pltpu.roll(t1, 1, 0)
                    d0, d1 = t0 - b0, t1 - jnp.where(sub == 0, b0, b1)
                    a0, a1 = pltpu.roll(d0, 7, 0), pltpu.roll(d1, 7, 0)
                    m0 = 0.5 * minmod(d0, jnp.where(sub == 7, a1, a0))
                    m1 = 0.5 * minmod(d1, jnp.where(sub == 7, 0.0, a1))
                    if positive:
                        u0, u1 = t0 + m0, t1 + m1
                        s0, s1 = pltpu.roll(u0, 1, 0), pltpu.roll(u1, 1, 0)
                        e0, e1 = u0 - jnp.where(sub < 2, 0.0, s0), u1 - jnp.where(sub == 0, s0, s1)
                    else:
                        u0, u1 = t0 - m0, t1 - m1
                        s0, s1 = pltpu.roll(u0, 7, 0), pltpu.roll(u1, 7, 0)
                        e0, e1 = jnp.where(sub == 7, s1, s0) - jnp.where(sub == 0, 0.0, u0), jnp.where(sub == 7, t1, s1) - u1
                    acc[x, h, r0] += cz0 * e0
                    acc[x, h, r1] += cz * e1
            return 0

        lax.fori_loop(0, 8, body, 0)

    pl.when(plus)(lambda: local_pass(True))
    pl.when(jnp.logical_not(plus))(lambda: local_pass(False))

    for cp in halo:
        cp.wait_recv()

    def x_pass(t, _):
        near, far = pl.ds(pl.multiple_of(t * 8, 8), 8), pl.ds(pl.multiple_of(t * 8 + 128, 8), 8)
        for h in range(2):
            for k, rows in enumerate((near, far)):
                low, high = xp[0, h, near], xp[1, h, near]
                if k:
                    low, high = pltpu.roll(low, 8, 1), pltpu.roll(high, 120, 1)
                v = [low, xf[0, h, rows]] + [g[x, h, rows] for x in range(8)] + [xf[1, h, rows], high]
                d = [v[i + 1] - v[i] for i in range(11)]
                half = [0.5 * minmod(d[i], d[i + 1]) for i in range(10)]
                face = [jnp.where(xpos, v[i + 1] + half[i], v[i + 2] - half[i + 1]) for i in range(9)]
                for x in range(8):
                    acc[x, h, rows] += step_x * (face[x + 1] - face[x])
        return 0

    lax.fori_loop(0, 16, x_pass, 0)

    weight = sum_weights(vz)

    def main_sums(x, _):
        mom[x] = sums(weight, joined(acc, x))
        return 0

    lax.fori_loop(0, 8, main_sums, 0)

    scatter = [remote(mom.at[(grp + o) % 8], rs.at[o], SCAT + o, peer(o)) for o in range(1, 8)]
    for cp in scatter:
        cp.start()

    def gather_wall(x, _):
        for l in range(2):
            for h in range(2):
                wm[h, x, pl.ds(l, 16, stride=2), :] = acc[x, h, pl.ds(l, 16, stride=16), :]
        return 0

    lax.fori_loop(0, 8, gather_wall, 0)
    pre[0] = sums(weight, flat(wm))
    early = remote(pre.at[0], pre.at[1], PRE, mirror)
    early.start()
    load_nu.wait()
    nu_main = spread(nu[grp], 16)
    nu_wall = spread(nu[...].reshape(128, 16), 2)
    basis = basis_table()

    total = mom[grp]
    for cp in scatter:
        cp.wait_recv()
    for o in range(1, 8):
        total = total + rs[o]
    zr[0] = total
    cross = remote(zr.at[0], zr.at[1], CROSS, across)
    cross.start()

    cross.wait_recv()
    rows = cell_values(total + zr[1], nu_main)
    par[grp] = jnp.concatenate(list(rows) + [jnp.zeros((7, 256), F32)], axis=0)
    gather = [remote(par.at[grp], par.at[grp], GATH + o, peer(o)) for o in range(1, 8)]
    for cp in gather:
        cp.start()
    for cp in wall:
        cp.wait_recv()
    step_wall = -DT * UNIT * jnp.abs(vz)

    def wall_pass(x, _):
        for h in range(2):
            v0, v1 = (g[x, h, pl.ds(l, 16, stride=16), :] for l in range(2))
            w0, w1 = wr[0, x, h], wr[1, x, h]
            p0, p1, m0, m1 = (jnp.where(plus, a, b) for a, b in ((v0, w0), (v1, w1), (w0, v0), (w1, v1)))
            jump = p0 - m0
            into = step_wall * (m0 - 0.5 * minmod(m1 - m0, -jump))
            out_of = step_wall * (p0 + 0.5 * minmod(jump, p1 - p0))
            dp[h, x, pl.ds(0, 16, stride=2), :] = out_of - into
            dp[h, x, pl.ds(1, 16, stride=2), :] = -out_of
            dm[h, x, pl.ds(0, 16, stride=2), :] = into
            dm[h, x, pl.ds(1, 16, stride=2), :] = jnp.zeros_like(into)
        return 0

    lax.fori_loop(0, 8, wall_pass, 0)
    plus_part, minus_part = flat(dp), flat(dm)
    early.wait_recv()
    part = sums(sum_weights(jnp.abs(vz)), plus_part) + sums(sum_weights(-jnp.abs(vz)), minus_part)
    cast[0] = part + (pre[0] + pre[1])
    casts = [remote(cast.at[0], cast.at[o], CAST + o, peer(o)) for o in range(1, 8)]
    for cp in casts:
        cp.start()
    beside = flat(wm) + jnp.where(plus, plus_part, minus_part)

    for cp in gather:
        cp.wait_recv()

    def main_relax(x, _):
        table = par[x]
        out[x] = relax([table[k : k + 1] for k in range(9)], basis, joined(acc, x), vz)
        return 0

    lax.fori_loop(0, 8, main_relax, 0)

    for cp in casts:
        cp.wait_recv()
    total = cast[0]
    for o in range(1, 8):
        total = total + cast[o]
    fixed = relax(cell_values(total, nu_wall), basis, beside, vz)
    for x in range(8):
        for k in range(16):
            out[x, k * 16 : k * 16 + 2, :] = fixed[x * 32 + k * 2 : x * 32 + k * 2 + 2]
    for cp in halo + wall + scatter + [cross, early] + gather + casts:
        cp.wait_send()


def shards(distribution, coefficients):
    cells = distribution.reshape(8, 256, 256)
    hbm = pl.BlockSpec(memory_space=pltpu.HBM)
    out = pl.pallas_call(
        kernel,
        out_shape=jax.ShapeDtypeStruct((8, 256, 256), F32),
        in_specs=[hbm, hbm],
        out_specs=pl.BlockSpec(memory_space=pltpu.VMEM),
        scratch_shapes=[
            pltpu.VMEM((8, 2, 256, 128), F32),
            pltpu.VMEM((8, 2, 256, 128), F32),
            pltpu.VMEM((8, 16, 16), F32),
            pltpu.VMEM((2, 2, 128, 128), F32),
            pltpu.VMEM((2, 2, 256, 128), F32),
            pltpu.VMEM((2, 2, 128, 128), F32),
            pltpu.VMEM((2, 8, 2, 16, 128), F32),
            pltpu.VMEM((2, 8, 2, 16, 128), F32),
            pltpu.VMEM((8, 16, 256), F32),
            pltpu.VMEM((8, 16, 256), F32),
            pltpu.VMEM((2, 16, 256), F32),
            pltpu.VMEM((8, 16, 256), F32),
            pltpu.VMEM((2, 8, 32, 128), F32),
            pltpu.VMEM((2, 8, 32, 128), F32),
            pltpu.VMEM((2, 8, 32, 128), F32),
            pltpu.VMEM((2, 16, 256), F32),
            pltpu.VMEM((8, 16, 256), F32),
            pltpu.SemaphoreType.DMA((COPIES,)),
            pltpu.SemaphoreType.DMA((COPIES,)),
            pltpu.SemaphoreType.DMA((8, 2)),
            pltpu.SemaphoreType.DMA,
        ],
        compiler_params=pltpu.CompilerParams(
            collective_id=0, has_side_effects=True, vmem_limit_bytes=40 * 1024 * 1024
        ),
        cost_estimate=pl.CostEstimate(flops=10**8, bytes_accessed=4 * 2**20, transcendentals=2**19),
    )(pltpu.with_memory_space_constraint(cells, pltpu.HBM), pltpu.with_memory_space_constraint(coefficients, pltpu.HBM))
    return out.reshape(distribution.shape)


def solution(mesh):
    in_specs = (P("vel", "space", None, None, None), P("space", None, None))
    out_specs = P("vel", "space", None, None, None)
    return jax.shard_map(shards, mesh=mesh, in_specs=in_specs, out_specs=out_specs, check_vma=False)
```

```python
import math

import jax
import jax.numpy as jnp
from jax import lax
from jax.experimental import pallas as pl
from jax.experimental.pallas import tpu as pltpu
from jax.sharding import PartitionSpec as P

NV = 16
UNIT = 0.3
DT = 0.035
WEIGHT = 0.6**3 / (2.0 * math.pi) ** 1.5
MESH = pl.DeviceIdType.MESH
F32 = jnp.float32
BF16 = jnp.bfloat16

HALO, WALL, SCAT, CROSS, GATH, CAST, COPIES = 0, 4, 8, 16, 17, 25, 33


def minmod(p, q):
    return jnp.maximum(jnp.minimum(p, q), 0.0) + jnp.minimum(jnp.maximum(p, q), 0.0)


def basis_table():
    row = lax.broadcasted_iota(jnp.int32, (32, 1024), 0)
    col = lax.broadcasted_iota(jnp.int32, (32, 1024), 1)
    b, block, k = col % 256, col // 256, row % 10
    x, y = (2 * (b % 16) - 15).astype(F32), (2 * (b // 16) - 15).astype(F32)
    value = jnp.where((k == 1) | (k == 6), x, 1.0)
    value = jnp.where((k == 2) | (k == 7), y, value)
    value = jnp.where(k == 3, x * x, jnp.where(k == 4, y * y, value))
    wanted = jnp.where(k < 5, 0, jnp.where(k < 8, 1, k - 6))
    return jnp.where((block == wanted) & (row < 30), value, 0.0).astype(BF16)


def spread(tile, width):
    k, c = (lax.broadcasted_iota(jnp.int32, (16, 256), d) for d in range(2))
    pick = jnp.where(c % width == k, 1.0, 0.0)
    wide = jnp.dot(tile, pick, precision=lax.Precision.HIGHEST, preferred_element_type=F32)
    r, c = (lax.broadcasted_iota(jnp.int32, wide.shape, d) for d in range(2))
    return jnp.sum(jnp.where(r == c // width, wide, 0.0), axis=0, keepdims=True)


def sum_weights(vz):
    row = lax.broadcasted_iota(jnp.int32, (16, 256), 0)
    b = lax.broadcasted_iota(jnp.int32, (16, 256), 1)
    x, y = (2 * (b % 16) - 15).astype(F32), (2 * (b // 16) - 15).astype(F32)
    z = jnp.zeros((16, 256), F32) + vz
    sq = x * x + y * y + z * z
    table = [jnp.ones_like(x), x, y, z, x * x, y * y, z * z, x * y, x * z, y * z, x * sq, y * sq, z * sq]
    weight = table[0]
    for k in range(1, 16):
        entry = table[k] if k < 13 else table[k - 3] - table[k - 3].astype(BF16).astype(F32)
        weight = jnp.where(row == k, entry, weight)
    return weight.astype(BF16)


def sums(weight, cells):
    hi = cells.astype(BF16)
    low = (cells - hi.astype(F32)).astype(BF16)
    dims = (((1,), (1,)), ((), ()))
    return lax.dot_general(weight, hi, dims, preferred_element_type=F32) + lax.dot_general(
        weight, low, dims, preferred_element_type=F32
    )


def joined(ref, x):
    return jnp.concatenate([ref[x, 0], ref[x, 1]], axis=1)


def flat(ref):
    return jnp.concatenate([ref[0].reshape(256, 128), ref[1].reshape(256, 128)], axis=1)


def cell_values(m, nu):
    mass, sx, sy, sz, xx, yy, zz, xy, xz, yz = m[:10]
    cx, cy, cz = (m[k] + m[k + 3] for k in range(10, 13))
    inv = 1.0 / mass
    ux, uy, uz = sx * inv, sy * inv, sz * inv
    energy = xx + yy + zz
    dot = ux * sx + uy * sy + uz * sz
    sq = ux * ux + uy * uy + uz * uz
    kinetic = energy - 2.0 * dot + sq * mass
    common = 2.0 * dot - energy - sq * mass
    fx = cx - 2.0 * (ux * xx + uy * xy + uz * xz) + ux * common + sq * sx
    fy = cy - 2.0 * (ux * xy + uy * yy + uz * yz) + uy * common + sq * sy
    fz = cz - 2.0 * (ux * xz + uy * yz + uz * zz) + uz * common + sq * sz
    temp = (UNIT * UNIT / 3.0) * kinetic * inv
    dens = WEIGHT * mass
    log_t = jnp.log(temp)
    decay = jnp.exp(-DT * nu * dens * jnp.exp((1.0 - 0.81) * log_t))
    inv_t = 1.0 / temp
    scale = (1.0 - decay) * dens * inv_t * lax.rsqrt(temp)
    skew = (1.0 - 2.0 / 3.0) / 5.0 * (0.5 * WEIGHT * UNIT**4) * scale / dens * inv_t * inv_t
    return ux, uy, uz, (UNIT * UNIT) * inv_t, scale, skew * fx, skew * fy, skew * fz, decay


def relax(rows, basis, moved, vz):
    ux, uy, uz, rt, scale, kx, ky, kz, decay = rows
    cz = vz - uz
    coef = [
        rt * (ux * ux + uy * uy + cz * cz),
        -2.0 * rt * ux,
        -2.0 * rt * uy,
        rt,
        rt,
        kz * cz - kx * ux - ky * uy,
        kx,
        ky,
        scale,
        decay,
    ]
    coef = jnp.concatenate(coef, axis=0)
    hi = coef.astype(BF16).astype(F32)
    mid = (coef - hi).astype(BF16).astype(F32)
    low = coef - hi - mid
    stacked = jnp.concatenate([hi, mid, low, jnp.zeros((2, coef.shape[1]), F32)], axis=0)
    left = stacked.T.astype(BF16)
    wide = jnp.dot(left, basis, preferred_element_type=F32)
    rr = wide[:, 0:256]
    return jnp.exp(-0.5 * rr) * (wide[:, 512:768] + wide[:, 256:512] * (rr - 5.0)) + moved * wide[:, 768:1024]


def kernel(f_hbm, nu_hbm, out, g, acc, nu, hp, xf, xp, ws, wr, mom, rs, zr, par, vals, freq, wm, dp, dm, cast, send, recv, local, nu_sem):
    vel, space = lax.axis_index("vel"), lax.axis_index("space")
    n_space = lax.axis_size("space")
    vy, zh, core = vel // 4, (vel // 2) % 2, vel % 2
    grp = vy * 2 + core

    def peer(o):
        p = (grp + o) % 8
        return {"vel": (p // 2) * 4 + zh * 2 + p % 2, "space": space}

    up = {"vel": vel, "space": (space + 1) % n_space}
    down = {"vel": vel, "space": (space + n_space - 1) % n_space}
    mirror = {"vel": NV - 1 - vel, "space": space}
    across = {"vel": vel + 2 - 4 * zh, "space": space}
    plus = vel >= NV // 2

    barrier = pltpu.get_barrier_semaphore()
    friends = [up, down, mirror, across] + [peer(o) for o in range(1, 8)]
    for d in friends:
        pl.semaphore_signal(barrier, inc=1, device_id=d, device_id_type=MESH)

    order = [0, 1, 6, 7, 2, 3, 4, 5]
    def halves(x):
        return [(f_hbm.at[x, :, pl.ds(h * 128, 128)], g.at[x, h], local.at[x, h]) for h in range(2)]

    loads = [[pltpu.make_async_copy(*c) for c in halves(x)] for x in range(8)]
    for x in order:
        for cp in loads[x]:
            cp.start()

    load_nu = pltpu.make_async_copy(nu_hbm, nu, nu_sem)
    load_nu.start()

    def remote(src, dst, k, dev):
        return pltpu.make_async_remote_copy(src, dst, send.at[k], recv.at[k], device_id=dev, device_id_type=MESH)

    vz = (2 * vel - 15).astype(F32)
    lane = lax.broadcasted_iota(jnp.int32, (8, 128), 1)
    sub = lax.broadcasted_iota(jnp.int32, (8, 128), 0)
    vx = (2 * (lane % 16) - 15).astype(F32)
    xpos = lane % 16 >= 8
    step_x = -DT * UNIT * vx
    step_y = [-DT * UNIT * (2 * (lane // 16 + 8 * h) - 15).astype(F32) for h in range(2)]

    for x in order[:4]:
        for cp in loads[x]:
            cp.wait()

    def pack(t, _):
        for h in range(2):
            near, far = pl.ds(pl.multiple_of(t * 8, 8), 8), pl.ds(pl.multiple_of(t * 8 + 128, 8), 8)
            hp[0, h, near] = jnp.where(xpos, g[6, h, near], pltpu.roll(g[6, h, far], 120, 1))
            hp[1, h, near] = jnp.where(xpos, pltpu.roll(g[1, h, far], 8, 1), g[1, h, near])
        return 0

    lax.fori_loop(0, 16, pack, 0)
    pl.semaphore_wait(barrier, len(friends))
    halo = [
        remote(g.at[7], xf.at[0], HALO, up),
        remote(hp.at[0], xp.at[0], HALO + 2, up),
        remote(g.at[0], xf.at[1], HALO + 1, down),
        remote(hp.at[1], xp.at[1], HALO + 3, down),
    ]
    for cp in halo:
        cp.start()
    for x in order[4:]:
        for cp in loads[x]:
            cp.wait()

    def pack_wall(x, _):
        for l in range(2):
            for h in range(2):
                ws[l, x, h] = g[x, h, pl.ds(l, 16, stride=16), :]
        return 0

    lax.fori_loop(0, 8, pack_wall, 0)
    wall = [remote(ws.at[l], wr.at[l], WALL + l, mirror) for l in range(2)]
    late = (space % 8 >= 3) & (space % 8 <= 4)

    def start_wall():
        for cp in wall:
            cp.start()

    pl.when(jnp.logical_not(late))(start_wall)

    def local_pass(positive):
        cz = -DT * UNIT * vz
        cz0 = jnp.where(sub < 1, 0.0, cz) if positive else cz

        def body(x, _):
            for h in range(2):
                for t in range(2):
                    v = [g[x, h, k * 16 + t * 8 : k * 16 + t * 8 + 8] for k in range(16)]
                    d = [v[k] - v[k - 1] for k in range(16)]
                    half = [0.5 * minmod(d[k], d[(k + 1) % 16]) for k in range(16)]
                    if h:
                        u = [v[k] + half[k] for k in range(16)]
                        change = [u[k] - u[k - 1] for k in range(16)]
                    else:
                        u = [v[k] - half[k] for k in range(16)]
                        change = [u[(k + 1) % 16] - u[k] for k in range(16)]
                    for k in range(16):
                        acc[x, h, k * 16 + t * 8 : k * 16 + t * 8 + 8] = v[k] + step_y[h] * change[k]
                for k in range(16):
                    r0, r1 = pl.ds(k * 16, 8), pl.ds(k * 16 + 8, 8)
                    t0, t1 = g[x, h, r0], g[x, h, r1]
                    b0, b1 = pltpu.roll(t0, 1, 0), pltpu.roll(t1, 1, 0)
                    d0, d1 = t0 - b0, t1 - jnp.where(sub == 0, b0, b1)
                    a0, a1 = pltpu.roll(d0, 7, 0), pltpu.roll(d1, 7, 0)
                    m0 = 0.5 * minmod(d0, jnp.where(sub == 7, a1, a0))
                    m1 = 0.5 * minmod(d1, jnp.where(sub == 7, 0.0, a1))
                    if positive:
                        u0, u1 = t0 + m0, t1 + m1
                        s0, s1 = pltpu.roll(u0, 1, 0), pltpu.roll(u1, 1, 0)
                        e0, e1 = u0 - jnp.where(sub < 2, 0.0, s0), u1 - jnp.where(sub == 0, s0, s1)
                    else:
                        u0, u1 = t0 - m0, t1 - m1
                        s0, s1 = pltpu.roll(u0, 7, 0), pltpu.roll(u1, 7, 0)
                        e0, e1 = jnp.where(sub == 7, s1, s0) - jnp.where(sub == 0, 0.0, u0), jnp.where(sub == 7, t1, s1) - u1
                    acc[x, h, r0] += cz0 * e0
                    acc[x, h, r1] += cz * e1
            return 0

        lax.fori_loop(0, 8, body, 0)

    pl.when(plus)(lambda: local_pass(True))
    pl.when(jnp.logical_not(plus))(lambda: local_pass(False))

    def x_inner(t, _):
        rows = pl.ds(pl.multiple_of(t * 8, 8), 8)
        for h in range(2):
            v = [g[x, h, rows] for x in range(8)]
            d = [v[i + 1] - v[i] for i in range(7)]
            half = [0.5 * minmod(d[i], d[i + 1]) for i in range(6)]
            face = [jnp.where(xpos, v[i + 1] + half[i], v[i + 2] - half[i + 1]) for i in range(5)]
            for x in range(4):
                acc[x + 2, h, rows] += step_x * (face[x + 1] - face[x])
        return 0

    lax.fori_loop(0, 32, x_inner, 0)
    weight = sum_weights(vz)

    def layer_sums(x):
        mom[x] = sums(weight, joined(acc, x))

    lax.fori_loop(2, 6, lambda x, _: (layer_sums(x), 0)[1], 0)
    load_nu.wait()

    def frequencies(x, _):
        freq[pl.ds(x, 1), :] = spread(nu[x], 16)
        return 0

    lax.fori_loop(0, 8, frequencies, 0)
    nu_wall = spread(nu[...].reshape(128, 16), 2)
    basis = basis_table()

    for cp in halo:
        cp.wait_recv()

    def x_outer(t, _):
        near, far = pl.ds(pl.multiple_of(t * 8, 8), 8), pl.ds(pl.multiple_of(t * 8 + 128, 8), 8)
        for h in range(2):
            for k, rows in enumerate((near, far)):
                low, high = xp[0, h, near], xp[1, h, near]
                if k:
                    low, high = pltpu.roll(low, 8, 1), pltpu.roll(high, 120, 1)
                below = [low, xf[0, h, rows]] + [g[x, h, rows] for x in range(4)]
                above = [g[x, h, rows] for x in range(4, 8)] + [xf[1, h, rows], high]
                for v, x0 in ((below, 0), (above, 6)):
                    d = [v[i + 1] - v[i] for i in range(5)]
                    half = [0.5 * minmod(d[i], d[i + 1]) for i in range(4)]
                    face = [jnp.where(xpos, v[i + 1] + half[i], v[i + 2] - half[i + 1]) for i in range(3)]
                    for x in range(2):
                        acc[x0 + x, h, rows] += step_x * (face[x + 1] - face[x])
        return 0

    lax.fori_loop(0, 16, x_outer, 0)
    lax.fori_loop(0, 4, lambda i, _: (layer_sums(i + 4 * (i // 2)), 0)[1], 0)

    scatter = [remote(mom.at[(grp + o) % 8], rs.at[o], SCAT + o, peer(o)) for o in range(1, 8)]
    for cp in scatter:
        cp.start()

    def gather_wall(x, _):
        for l in range(2):
            for h in range(2):
                wm[h, x, pl.ds(l, 16, stride=2), :] = acc[x, h, pl.ds(l, 16, stride=16), :]
        return 0

    lax.fori_loop(0, 8, gather_wall, 0)
    total = mom[grp]
    for cp in scatter:
        cp.wait_recv()
    for o in range(1, 8):
        total = total + rs[o]
    zr[0] = total
    cross = remote(zr.at[0], zr.at[1], CROSS, across)
    cross.start()
    pl.when(late)(start_wall)

    cross.wait_recv()
    total = total + zr[1]
    own = pl.ds(pl.multiple_of(grp * 16, 16), 16)
    for h in range(2):
        par[h, own, :] = total[:, h * 128 : h * 128 + 128]
    gather = [remote(par.at[:, own, :], par.at[:, own, :], GATH + o, peer(o)) for o in range(1, 8)]
    for cp in gather:
        cp.start()

    for cp in wall:
        cp.wait_recv()
    step_wall = -DT * UNIT * jnp.abs(vz)

    def wall_pass(x, _):
        for h in range(2):
            v0, v1 = (g[x, h, pl.ds(l, 16, stride=16), :] for l in range(2))
            w0, w1 = wr[0, x, h], wr[1, x, h]
            p0, p1, m0, m1 = (jnp.where(plus, a, b) for a, b in ((v0, w0), (v1, w1), (w0, v0), (w1, v1)))
            jump = p0 - m0
            into = step_wall * (m0 - 0.5 * minmod(m1 - m0, -jump))
            out_of = step_wall * (p0 + 0.5 * minmod(jump, p1 - p0))
            dp[h, x, pl.ds(0, 16, stride=2), :] = out_of - into
            dp[h, x, pl.ds(1, 16, stride=2), :] = -out_of
            dm[h, x, pl.ds(0, 16, stride=2), :] = into
            dm[h, x, pl.ds(1, 16, stride=2), :] = jnp.zeros_like(into)
        return 0

    lax.fori_loop(0, 8, wall_pass, 0)
    plus_part, minus_part = flat(dp), flat(dm)
    cast[0] = sums(sum_weights(jnp.abs(vz)), plus_part) + sums(sum_weights(-jnp.abs(vz)), minus_part)
    casts = [remote(cast.at[0], cast.at[o], CAST + o, peer(o)) for o in range(1, 8)]
    for cp in casts:
        cp.start()
    beside = flat(wm) + jnp.where(plus, plus_part, minus_part)

    for cp in gather:
        cp.wait_recv()

    def strided(k):
        return jnp.concatenate([par[h, pl.ds(k, 8, stride=16), :] for h in range(2)], axis=1)

    for k, row in enumerate(cell_values([strided(k) for k in range(16)], freq[...])):
        vals[k] = row

    def main_relax(x, _):
        out[x] = relax([vals[k, pl.ds(x, 1), :] for k in range(9)], basis, joined(acc, x), vz)
        return 0

    lax.fori_loop(0, 8, main_relax, 0)

    r, c = (lax.broadcasted_iota(jnp.int32, (256, 32), d) for d in range(2))
    pick = jnp.where(r == (c // 2) * 16 + c % 2, 1.0, 0.0)
    wall_sums = []
    for x in range(8):
        layer = jnp.concatenate([par[h, x * 16 : x * 16 + 16, :] for h in range(2)], axis=1)
        wall_sums.append(jnp.dot(layer, pick, precision=lax.Precision.HIGHEST, preferred_element_type=F32))
    total = jnp.concatenate(wall_sums, axis=1)
    for cp in casts:
        cp.wait_recv()
    for o in range(8):
        total = total + cast[o]
    fixed = relax(cell_values([total[k : k + 1] for k in range(16)], nu_wall), basis, beside, vz)
    for x in range(8):
        for k in range(16):
            out[x, k * 16 : k * 16 + 2, :] = fixed[x * 32 + k * 2 : x * 32 + k * 2 + 2]
    for cp in halo + wall + scatter + [cross] + gather + casts:
        cp.wait_send()


def shards(distribution, coefficients):
    cells = distribution.reshape(8, 256, 256)
    hbm = pl.BlockSpec(memory_space=pltpu.HBM)
    out = pl.pallas_call(
        kernel,
        out_shape=jax.ShapeDtypeStruct((8, 256, 256), F32),
        in_specs=[hbm, hbm],
        out_specs=pl.BlockSpec(memory_space=pltpu.VMEM),
        scratch_shapes=[
            pltpu.VMEM((8, 2, 256, 128), F32),
            pltpu.VMEM((8, 2, 256, 128), F32),
            pltpu.VMEM((8, 16, 16), F32),
            pltpu.VMEM((2, 2, 128, 128), F32),
            pltpu.VMEM((2, 2, 256, 128), F32),
            pltpu.VMEM((2, 2, 128, 128), F32),
            pltpu.VMEM((2, 8, 2, 16, 128), F32),
            pltpu.VMEM((2, 8, 2, 16, 128), F32),
            pltpu.VMEM((8, 16, 256), F32),
            pltpu.VMEM((8, 16, 256), F32),
            pltpu.VMEM((2, 16, 256), F32),
            pltpu.VMEM((2, 128, 128), F32),
            pltpu.VMEM((9, 8, 256), F32),
            pltpu.VMEM((8, 256), F32),
            pltpu.VMEM((2, 8, 32, 128), F32),
            pltpu.VMEM((2, 8, 32, 128), F32),
            pltpu.VMEM((2, 8, 32, 128), F32),
            pltpu.VMEM((8, 16, 256), F32),
            pltpu.SemaphoreType.DMA((COPIES,)),
            pltpu.SemaphoreType.DMA((COPIES,)),
            pltpu.SemaphoreType.DMA((8, 2)),
            pltpu.SemaphoreType.DMA,
        ],
        compiler_params=pltpu.CompilerParams(
            collective_id=0, has_side_effects=True, vmem_limit_bytes=40 * 1024 * 1024
        ),
        cost_estimate=pl.CostEstimate(flops=10**8, bytes_accessed=4 * 2**20, transcendentals=2**19),
    )(pltpu.with_memory_space_constraint(cells, pltpu.HBM), pltpu.with_memory_space_constraint(coefficients, pltpu.HBM))
    return out.reshape(distribution.shape)


def solution(mesh):
    in_specs = (P("vel", "space", None, None, None), P("space", None, None))
    out_specs = P("vel", "space", None, None, None)
    return jax.shard_map(shards, mesh=mesh, in_specs=in_specs, out_specs=out_specs, check_vma=False)
```

```python
import math

import jax
import jax.numpy as jnp
from jax import lax
from jax.experimental import pallas as pl
from jax.experimental.pallas import tpu as pltpu
from jax.sharding import PartitionSpec as P

NV = 16
UNIT = 0.3
DT = 0.035
WEIGHT = 0.6**3 / (2.0 * math.pi) ** 1.5
MESH = pl.DeviceIdType.MESH
F32 = jnp.float32
BF16 = jnp.bfloat16

HALO, WALL, SCAT, CROSS, GATH, CAST, COPIES = 0, 4, 8, 16, 17, 25, 33


def minmod(p, q):
    return jnp.maximum(jnp.minimum(p, q), 0.0) + jnp.minimum(jnp.maximum(p, q), 0.0)


def basis_table():
    row = lax.broadcasted_iota(jnp.int32, (32, 1024), 0)
    col = lax.broadcasted_iota(jnp.int32, (32, 1024), 1)
    b, block, k = col % 256, col // 256, row % 10
    x, y = (2 * (b % 16) - 15).astype(F32), (2 * (b // 16) - 15).astype(F32)
    value = jnp.where((k == 1) | (k == 6), x, 1.0)
    value = jnp.where((k == 2) | (k == 7), y, value)
    value = jnp.where(k == 3, x * x, jnp.where(k == 4, y * y, value))
    wanted = jnp.where(k < 5, 0, jnp.where(k < 8, 1, k - 6))
    return jnp.where((block == wanted) & (row < 30), value, 0.0).astype(BF16)


def spread(tile, width):
    k, c = (lax.broadcasted_iota(jnp.int32, (16, 256), d) for d in range(2))
    pick = jnp.where(c % width == k, 1.0, 0.0)
    wide = jnp.dot(tile, pick, precision=lax.Precision.HIGHEST, preferred_element_type=F32)
    r, c = (lax.broadcasted_iota(jnp.int32, wide.shape, d) for d in range(2))
    return jnp.sum(jnp.where(r == c // width, wide, 0.0), axis=0, keepdims=True)


def sum_weights(vz):
    row = lax.broadcasted_iota(jnp.int32, (16, 256), 0)
    b = lax.broadcasted_iota(jnp.int32, (16, 256), 1)
    x, y = (2 * (b % 16) - 15).astype(F32), (2 * (b // 16) - 15).astype(F32)
    z = jnp.zeros((16, 256), F32) + vz
    sq = x * x + y * y + z * z
    table = [jnp.ones_like(x), x, y, z, x * x, y * y, z * z, x * y, x * z, y * z, x * sq, y * sq, z * sq]
    weight = table[0]
    for k in range(1, 16):
        entry = table[k] if k < 13 else table[k - 3] - table[k - 3].astype(BF16).astype(F32)
        weight = jnp.where(row == k, entry, weight)
    return weight.astype(BF16)


def sums(weight, cells):
    hi = cells.astype(BF16)
    low = (cells - hi.astype(F32)).astype(BF16)
    dims = (((1,), (1,)), ((), ()))
    return lax.dot_general(weight, hi, dims, preferred_element_type=F32) + lax.dot_general(
        weight, low, dims, preferred_element_type=F32
    )


def joined(ref, x):
    return jnp.concatenate([ref[x, 0], ref[x, 1]], axis=1)


def flat(ref):
    return jnp.concatenate([ref[0].reshape(256, 128), ref[1].reshape(256, 128)], axis=1)


def cell_values(m, nu):
    mass, sx, sy, sz, xx, yy, zz, xy, xz, yz = m[:10]
    cx, cy, cz = (m[k] + m[k + 3] for k in range(10, 13))
    inv = 1.0 / mass
    ux, uy, uz = sx * inv, sy * inv, sz * inv
    energy = xx + yy + zz
    dot = ux * sx + uy * sy + uz * sz
    sq = ux * ux + uy * uy + uz * uz
    kinetic = energy - 2.0 * dot + sq * mass
    common = 2.0 * dot - energy - sq * mass
    fx = cx - 2.0 * (ux * xx + uy * xy + uz * xz) + ux * common + sq * sx
    fy = cy - 2.0 * (ux * xy + uy * yy + uz * yz) + uy * common + sq * sy
    fz = cz - 2.0 * (ux * xz + uy * yz + uz * zz) + uz * common + sq * sz
    temp = (UNIT * UNIT / 3.0) * kinetic * inv
    dens = WEIGHT * mass
    log_t = jnp.log(temp)
    decay = jnp.exp(-DT * nu * dens * jnp.exp((1.0 - 0.81) * log_t))
    inv_t = 1.0 / temp
    scale = (1.0 - decay) * dens * inv_t * lax.rsqrt(temp)
    skew = (1.0 - 2.0 / 3.0) / 5.0 * (0.5 * WEIGHT * UNIT**4) * scale / dens * inv_t * inv_t
    return ux, uy, uz, (UNIT * UNIT) * inv_t, scale, skew * fx, skew * fy, skew * fz, decay


def relax(rows, basis, moved, vz):
    ux, uy, uz, rt, scale, kx, ky, kz, decay = rows
    cz = vz - uz
    coef = [
        rt * (ux * ux + uy * uy + cz * cz),
        -2.0 * rt * ux,
        -2.0 * rt * uy,
        rt,
        rt,
        kz * cz - kx * ux - ky * uy,
        kx,
        ky,
        scale,
        decay,
    ]
    coef = jnp.concatenate(coef, axis=0)
    hi = coef.astype(BF16).astype(F32)
    mid = (coef - hi).astype(BF16).astype(F32)
    low = coef - hi - mid
    stacked = jnp.concatenate([hi, mid, low, jnp.zeros((2, coef.shape[1]), F32)], axis=0)
    left = stacked.T.astype(BF16)
    wide = jnp.dot(left, basis, preferred_element_type=F32)
    rr = wide[:, 0:256]
    return jnp.exp(-0.5 * rr) * (wide[:, 512:768] + wide[:, 256:512] * (rr - 5.0)) + moved * wide[:, 768:1024]


def kernel(f_hbm, nu_hbm, out, g, acc, nu, hp, xf, xp, ws, wr, mom, rs, zr, par, vals, freq, wm, dp, dm, cast, send, recv, local, nu_sem):
    vel, space = lax.axis_index("vel"), lax.axis_index("space")
    n_space = lax.axis_size("space")
    vy, zh, core = vel // 4, (vel // 2) % 2, vel % 2
    grp = vy * 2 + core

    def peer(o):
        p = (grp + o) % 8
        return {"vel": (p // 2) * 4 + zh * 2 + p % 2, "space": space}

    up = {"vel": vel, "space": (space + 1) % n_space}
    down = {"vel": vel, "space": (space + n_space - 1) % n_space}
    mirror = {"vel": NV - 1 - vel, "space": space}
    across = {"vel": vel + 2 - 4 * zh, "space": space}
    plus = vel >= NV // 2

    barrier = pltpu.get_barrier_semaphore()
    friends = [up, down, mirror, across] + [peer(o) for o in range(1, 8)]
    for d in friends:
        pl.semaphore_signal(barrier, inc=1, device_id=d, device_id_type=MESH)

    order = [0, 1, 6, 7, 2, 3, 4, 5]
    def halves(x):
        return [(f_hbm.at[x, :, pl.ds(h * 128, 128)], g.at[x, h], local.at[x, h]) for h in range(2)]

    loads = [[pltpu.make_async_copy(*c) for c in halves(x)] for x in range(8)]
    for x in order:
        for cp in loads[x]:
            cp.start()

    load_nu = pltpu.make_async_copy(nu_hbm, nu, nu_sem)
    load_nu.start()

    def remote(src, dst, k, dev):
        return pltpu.make_async_remote_copy(src, dst, send.at[k], recv.at[k], device_id=dev, device_id_type=MESH)

    vz = (2 * vel - 15).astype(F32)
    lane = lax.broadcasted_iota(jnp.int32, (8, 128), 1)
    sub = lax.broadcasted_iota(jnp.int32, (8, 128), 0)
    vx = (2 * (lane % 16) - 15).astype(F32)
    xpos = lane % 16 >= 8
    step_x = -DT * UNIT * vx
    step_y = [-DT * UNIT * (2 * (lane // 16 + 8 * h) - 15).astype(F32) for h in range(2)]

    for x in order[:4]:
        for cp in loads[x]:
            cp.wait()

    def pack(t, _):
        for h in range(2):
            near, far = pl.ds(pl.multiple_of(t * 8, 8), 8), pl.ds(pl.multiple_of(t * 8 + 128, 8), 8)
            hp[0, h, near] = jnp.where(xpos, g[6, h, near], pltpu.roll(g[6, h, far], 120, 1))
            hp[1, h, near] = jnp.where(xpos, pltpu.roll(g[1, h, far], 8, 1), g[1, h, near])
        return 0

    lax.fori_loop(0, 16, pack, 0)
    pl.semaphore_wait(barrier, len(friends))
    halo = [
        remote(g.at[7], xf.at[0], HALO, up),
        remote(hp.at[0], xp.at[0], HALO + 2, up),
        remote(g.at[0], xf.at[1], HALO + 1, down),
        remote(hp.at[1], xp.at[1], HALO + 3, down),
    ]
    for cp in halo:
        cp.start()
    for x in order[4:]:
        for cp in loads[x]:
            cp.wait()

    def pack_wall(x, _):
        for l in range(2):
            for h in range(2):
                ws[l, x, h] = g[x, h, pl.ds(l, 16, stride=16), :]
        return 0

    lax.fori_loop(0, 8, pack_wall, 0)
    wall = [remote(ws.at[l], wr.at[l], WALL + l, mirror) for l in range(2)]
    late = (space % 8 >= 3) & (space % 8 <= 4)

    def start_wall():
        for cp in wall:
            cp.start()

    pl.when(jnp.logical_not(late))(start_wall)

    def local_pass(positive):
        cz = -DT * UNIT * vz
        cz0 = jnp.where(sub < 1, 0.0, cz) if positive else cz

        def body(x, _):
            for h in range(2):
                for t in range(2):
                    v = [g[x, h, k * 16 + t * 8 : k * 16 + t * 8 + 8] for k in range(16)]
                    d = [v[k] - v[k - 1] for k in range(16)]
                    half = [0.5 * minmod(d[k], d[(k + 1) % 16]) for k in range(16)]
                    if h:
                        u = [v[k] + half[k] for k in range(16)]
                        change = [u[k] - u[k - 1] for k in range(16)]
                    else:
                        u = [v[k] - half[k] for k in range(16)]
                        change = [u[(k + 1) % 16] - u[k] for k in range(16)]
                    for k in range(16):
                        acc[x, h, k * 16 + t * 8 : k * 16 + t * 8 + 8] = v[k] + step_y[h] * change[k]
                for k in range(16):
                    r0, r1 = pl.ds(k * 16, 8), pl.ds(k * 16 + 8, 8)
                    t0, t1 = g[x, h, r0], g[x, h, r1]
                    b0, b1 = pltpu.roll(t0, 1, 0), pltpu.roll(t1, 1, 0)
                    d0, d1 = t0 - b0, t1 - jnp.where(sub == 0, b0, b1)
                    a0, a1 = pltpu.roll(d0, 7, 0), pltpu.roll(d1, 7, 0)
                    m0 = 0.5 * minmod(d0, jnp.where(sub == 7, a1, a0))
                    m1 = 0.5 * minmod(d1, jnp.where(sub == 7, 0.0, a1))
                    if positive:
                        u0, u1 = t0 + m0, t1 + m1
                        s0, s1 = pltpu.roll(u0, 1, 0), pltpu.roll(u1, 1, 0)
                        e0, e1 = u0 - jnp.where(sub < 2, 0.0, s0), u1 - jnp.where(sub == 0, s0, s1)
                    else:
                        u0, u1 = t0 - m0, t1 - m1
                        s0, s1 = pltpu.roll(u0, 7, 0), pltpu.roll(u1, 7, 0)
                        e0, e1 = jnp.where(sub == 7, s1, s0) - jnp.where(sub == 0, 0.0, u0), jnp.where(sub == 7, t1, s1) - u1
                    acc[x, h, r0] += cz0 * e0
                    acc[x, h, r1] += cz * e1
            return 0

        lax.fori_loop(0, 8, body, 0)

    pl.when(plus)(lambda: local_pass(True))
    pl.when(jnp.logical_not(plus))(lambda: local_pass(False))

    def x_inner(t, _):
        rows = pl.ds(pl.multiple_of(t * 8, 8), 8)
        for h in range(2):
            v = [g[x, h, rows] for x in range(8)]
            d = [v[i + 1] - v[i] for i in range(7)]
            half = [0.5 * minmod(d[i], d[i + 1]) for i in range(6)]
            face = [jnp.where(xpos, v[i + 1] + half[i], v[i + 2] - half[i + 1]) for i in range(5)]
            for x in range(4):
                acc[x + 2, h, rows] += step_x * (face[x + 1] - face[x])
        return 0

    lax.fori_loop(0, 32, x_inner, 0)
    weight = sum_weights(vz)

    def layer_sums(x):
        mom[x] = sums(weight, joined(acc, x))

    lax.fori_loop(2, 6, lambda x, _: (layer_sums(x), 0)[1], 0)
    load_nu.wait()

    def frequencies(x, _):
        freq[pl.ds(x, 1), :] = spread(nu[x], 16)
        return 0

    lax.fori_loop(0, 8, frequencies, 0)
    nu_wall = spread(nu[...].reshape(128, 16), 2)
    basis = basis_table()

    for cp in halo:
        cp.wait_recv()

    def x_outer(t, _):
        near, far = pl.ds(pl.multiple_of(t * 8, 8), 8), pl.ds(pl.multiple_of(t * 8 + 128, 8), 8)
        for h in range(2):
            for k, rows in enumerate((near, far)):
                low, high = xp[0, h, near], xp[1, h, near]
                if k:
                    low, high = pltpu.roll(low, 8, 1), pltpu.roll(high, 120, 1)
                below = [low, xf[0, h, rows]] + [g[x, h, rows] for x in range(4)]
                above = [g[x, h, rows] for x in range(4, 8)] + [xf[1, h, rows], high]
                for v, x0 in ((below, 0), (above, 6)):
                    d = [v[i + 1] - v[i] for i in range(5)]
                    half = [0.5 * minmod(d[i], d[i + 1]) for i in range(4)]
                    face = [jnp.where(xpos, v[i + 1] + half[i], v[i + 2] - half[i + 1]) for i in range(3)]
                    for x in range(2):
                        acc[x0 + x, h, rows] += step_x * (face[x + 1] - face[x])
        return 0

    lax.fori_loop(0, 16, x_outer, 0)
    lax.fori_loop(0, 4, lambda i, _: (layer_sums(i + 4 * (i // 2)), 0)[1], 0)

    scatter = [remote(mom.at[(grp + o) % 8], rs.at[o], SCAT + o, peer(o)) for o in range(1, 8)]
    for cp in scatter:
        cp.start()

    def gather_wall(x, _):
        for l in range(2):
            for h in range(2):
                wm[h, x, pl.ds(l, 16, stride=2), :] = acc[x, h, pl.ds(l, 16, stride=16), :]
        return 0

    lax.fori_loop(0, 8, gather_wall, 0)
    total = mom[grp]
    for cp in scatter:
        cp.wait_recv()
    for o in range(1, 8):
        total = total + rs[o]
    zr[0] = total
    cross = remote(zr.at[0], zr.at[1], CROSS, across)
    cross.start()
    pl.when(late)(start_wall)

    cross.wait_recv()
    total = total + zr[1]
    own = pl.ds(pl.multiple_of(grp * 16, 16), 16)
    for h in range(2):
        par[h, own, :] = total[:, h * 128 : h * 128 + 128]
    gather = [remote(par.at[:, own, :], par.at[:, own, :], GATH + o, peer(o)) for o in range(1, 8)]
    for cp in gather:
        cp.start()

    for cp in wall:
        cp.wait_recv()
    step_wall = -DT * UNIT * jnp.abs(vz)

    def wall_pass(x, _):
        for h in range(2):
            v0, v1 = (g[x, h, pl.ds(l, 16, stride=16), :] for l in range(2))
            w0, w1 = wr[0, x, h], wr[1, x, h]
            p0, p1, m0, m1 = (jnp.where(plus, a, b) for a, b in ((v0, w0), (v1, w1), (w0, v0), (w1, v1)))
            jump = p0 - m0
            into = step_wall * (m0 - 0.5 * minmod(m1 - m0, -jump))
            out_of = step_wall * (p0 + 0.5 * minmod(jump, p1 - p0))
            dp[h, x, pl.ds(0, 16, stride=2), :] = out_of - into
            dp[h, x, pl.ds(1, 16, stride=2), :] = -out_of
            dm[h, x, pl.ds(0, 16, stride=2), :] = into
            dm[h, x, pl.ds(1, 16, stride=2), :] = jnp.zeros_like(into)
        return 0

    lax.fori_loop(0, 8, wall_pass, 0)
    plus_part, minus_part = flat(dp), flat(dm)
    cast[0] = sums(sum_weights(jnp.abs(vz)), plus_part) + sums(sum_weights(-jnp.abs(vz)), minus_part)
    casts = [remote(cast.at[0], cast.at[o], CAST + o, peer(o)) for o in range(1, 8)]
    for cp in casts:
        cp.start()
    beside = flat(wm) + jnp.where(plus, plus_part, minus_part)

    for cp in gather:
        cp.wait_recv()

    def strided(k):
        return jnp.concatenate([par[h, pl.ds(k, 8, stride=16), :] for h in range(2)], axis=1)

    for k, row in enumerate(cell_values([strided(k) for k in range(16)], freq[...])):
        vals[k] = row

    def main_relax(x, _):
        out[x] = relax([vals[k, pl.ds(x, 1), :] for k in range(9)], basis, joined(acc, x), vz)
        return 0

    lax.fori_loop(0, 8, main_relax, 0)

    r, c = (lax.broadcasted_iota(jnp.int32, (256, 32), d) for d in range(2))
    pick = jnp.where(r == (c // 2) * 16 + c % 2, 1.0, 0.0)
    every = jnp.concatenate([par[0], par[1]], axis=1)
    picked = jnp.dot(every, pick, precision=lax.Precision.HIGHEST, preferred_element_type=F32)
    total = jnp.concatenate([picked[x * 16 : x * 16 + 16] for x in range(8)], axis=1)
    for cp in casts:
        cp.wait_recv()
    for o in range(8):
        total = total + cast[o]
    fixed = relax(cell_values([total[k : k + 1] for k in range(16)], nu_wall), basis, beside, vz)
    for x in range(8):
        for k in range(16):
            out[x, k * 16 : k * 16 + 2, :] = fixed[x * 32 + k * 2 : x * 32 + k * 2 + 2]
    for cp in halo + wall + scatter + [cross] + gather + casts:
        cp.wait_send()


def shards(distribution, coefficients):
    cells = distribution.reshape(8, 256, 256)
    hbm = pl.BlockSpec(memory_space=pltpu.HBM)
    out = pl.pallas_call(
        kernel,
        out_shape=jax.ShapeDtypeStruct((8, 256, 256), F32),
        in_specs=[hbm, hbm],
        out_specs=pl.BlockSpec(memory_space=pltpu.VMEM),
        scratch_shapes=[
            pltpu.VMEM((8, 2, 256, 128), F32),
            pltpu.VMEM((8, 2, 256, 128), F32),
            pltpu.VMEM((8, 16, 16), F32),
            pltpu.VMEM((2, 2, 128, 128), F32),
            pltpu.VMEM((2, 2, 256, 128), F32),
            pltpu.VMEM((2, 2, 128, 128), F32),
            pltpu.VMEM((2, 8, 2, 16, 128), F32),
            pltpu.VMEM((2, 8, 2, 16, 128), F32),
            pltpu.VMEM((8, 16, 256), F32),
            pltpu.VMEM((8, 16, 256), F32),
            pltpu.VMEM((2, 16, 256), F32),
            pltpu.VMEM((2, 128, 128), F32),
            pltpu.VMEM((9, 8, 256), F32),
            pltpu.VMEM((8, 256), F32),
            pltpu.VMEM((2, 8, 32, 128), F32),
            pltpu.VMEM((2, 8, 32, 128), F32),
            pltpu.VMEM((2, 8, 32, 128), F32),
            pltpu.VMEM((8, 16, 256), F32),
            pltpu.SemaphoreType.DMA((COPIES,)),
            pltpu.SemaphoreType.DMA((COPIES,)),
            pltpu.SemaphoreType.DMA((8, 2)),
            pltpu.SemaphoreType.DMA,
        ],
        compiler_params=pltpu.CompilerParams(
            collective_id=0, has_side_effects=True, vmem_limit_bytes=40 * 1024 * 1024
        ),
        cost_estimate=pl.CostEstimate(flops=10**8, bytes_accessed=4 * 2**20, transcendentals=2**19),
    )(pltpu.with_memory_space_constraint(cells, pltpu.HBM), pltpu.with_memory_space_constraint(coefficients, pltpu.HBM))
    return out.reshape(distribution.shape)


def solution(mesh):
    in_specs = (P("vel", "space", None, None, None), P("space", None, None))
    out_specs = P("vel", "space", None, None, None)
    return jax.shard_map(shards, mesh=mesh, in_specs=in_specs, out_specs=out_specs, check_vma=False)
```
